32 devices in a mesh: groups: 2 (over y), lon: 4 (over z), lat: 4 (over x, core).
Axes of the slice: x: 2, y: 2, z: 4, core: 2. Of those that a mesh axis runs over, the one named last changes fastest.
Arguments:
- latent: bfloat16 [4, 96, 128, 320], P('groups', 'lat', 'lon'), parts along dimension 0, may hold values from -27 to 27
- band_index: int32 [96], P('lat'), may hold values from 0 to 7
- time_shift: float32 [4, 320], P('groups'), parts along dimension 0, may hold values from -4 to 4
- norm_gains: float32 [2, 320], replicated, may hold values from 0.1 to 1.9
- tap_scale: float32 [2, 8, 9, 320], replicated, may hold values from 0.5 to 2
- conv_one: bfloat16 [9, 320, 320], replicated, may hold values from -0.109375 to 0.109375
- conv_two: bfloat16 [9, 320, 320], replicated, may hold values from -0.109375 to 0.109375
Outputs:
- block_out: bfloat16 [4, 96, 128, 320], P('groups', 'lat', 'lon'), parts along dimension 0
The draws below stay inside these ranges and needn't reach their ends.
There are 2 independent parts, one for each index of `groups`. The reference program is written for one: setup_inputs(seed, part) draws one part's arguments, and reference() takes and returns one part's arrays. A program takes and returns all parts, laid end to end along the dimension named above; an argument that names none is the same for every part. Nothing has to cross between parts.
All inputs are finite; a program needn't handle non-finite values.
Results may differ from the reference program's by a relative error of at most 0.0037.
Values may be sent and summed in bfloat16 or wider, within the bound.
A program may use at most 64 MiB of HBM per device.

```python
import math
import jax
import jax.numpy as jnp
from jax import lax

C = 320
NORM_GROUPS = 32
B = 2
NB = 8
H = 96
W = 128


def group_offsets(key, low, high):
    size_key, sign_key = jax.random.split(key)
    magnitude = jax.random.uniform(size_key, (B, NORM_GROUPS), jnp.float32, low, high)
    signs = 2.0 * jax.random.randint(sign_key, (B, NORM_GROUPS), 0, 2).astype(jnp.float32) - 1.0
    offsets = jnp.repeat(magnitude * signs, C // NORM_GROUPS, axis=1)
    return offsets[:, None, None, :]


def draw_latent(key, part):
    key = jax.random.fold_in(key, 11)
    base_key, rough_key, offset_key, phase_key = jax.random.split(key, 4)
    rows_pos = jnp.arange(H, dtype=jnp.float32) / H
    cols_pos = jnp.arange(W, dtype=jnp.float32) / W
    rough = jax.random.uniform(rough_key, (B, H, W, C), jnp.float32, 0.6, 1.4)
    phases = jax.random.uniform(phase_key, (B,), jnp.float32, 0.0, 1.0)
    lon_pos = jnp.mod(cols_pos[None, :] + phases[:, None], 1.0)
    falling = (jnp.arange(B) % 2 == 1)[:, None]
    lon_pos = jnp.where(falling, 1.0 - lon_pos, lon_pos)
    lon_factor = jnp.exp(jnp.log(3.0) * lon_pos)
    base = 0.42 * (jax.random.truncated_normal(base_key, -4.0, 4.0, (B, H, W, C), jnp.float32) + group_offsets(offset_key, 0.4, 0.8))
    lat_factor = jnp.exp(jnp.log(3.0) * rows_pos)
    return (base * rough * lat_factor[None, :, None, None] * lon_factor[:, None, :, None]).astype(jnp.bfloat16)


def plant(entries, key, smallest, high):
    spot = [jax.random.randint(jax.random.fold_in(key, axis), (), 0, length) for axis, length in enumerate(entries.shape)]
    longest = entries.shape.index(max(entries.shape))
    next_to = spot[:longest] + [(spot[longest] + 1) % entries.shape[longest]] + spot[longest + 1:]
    return entries.at[tuple(spot)].set(smallest).at[tuple(next_to)].set(high)


def gaussian(own_key, extent, deviation, bound, held_as=jnp.bfloat16):
    return jnp.clip(deviation * jax.random.normal(own_key, extent, jnp.float32), -bound, bound).astype(held_as)


def setup_inputs(seed: int = 0, part: int = 0) -> dict:
    key_of = jax.random.split(jax.random.key(seed), 8)
    part_keys = jax.random.split(jax.random.fold_in(key_of[7], part), 8)
    return {
        "latent": draw_latent(jax.random.fold_in(jax.random.fold_in(key_of[7], part), 71), part),
        "band_index": plant(jax.random.randint(key_of[1], (H,), 0, NB), jax.random.fold_in(key_of[1], 1), 0, NB - 1).astype(jnp.int32),
        "time_shift": gaussian(part_keys[2], (B, C), 1.0, 4.0, jnp.float32),
        "norm_gains": jnp.clip(1.0 + 0.18 * jax.random.normal(key_of[3], (2, C), jnp.float32), 0.1, 1.9),
        "tap_scale": jnp.clip(jnp.exp(jax.random.uniform(key_of[4], (2, NB, 9, C), jnp.float32, math.log(0.5), math.log(2.0))), 0.5, 2.0),
        "conv_one": gaussian(key_of[5], (9, C, C), (9 * C) ** -0.5, 0.109375),
        "conv_two": gaussian(key_of[6], (9, C, C), (9 * C) ** -0.5, 0.109375),
    }


EPSILON = 1e-06

def norm_silu(field, gain):
    batch, rows_lat, cols_lon, chans = field.shape
    grouped = field.reshape(batch, rows_lat, cols_lon, NORM_GROUPS, chans // NORM_GROUPS)
    average = lax.optimization_barrier(jnp.mean(grouped, axis=(1, 2, 4), keepdims=True))
    spread = lax.optimization_barrier(jnp.mean(jnp.square(grouped - average), axis=(1, 2, 4), keepdims=True))
    normed = ((grouped - average) * lax.rsqrt(spread + EPSILON)).reshape(batch, rows_lat, cols_lon, chans)
    return jax.nn.silu(normed * gain).astype(jnp.bfloat16)

def convolve(activation, kernel, row_scales):
    batch, rows_lat, cols_lon, chans = activation.shape
    padded = jnp.pad(activation, ((0, 0), (1, 1), (0, 0), (0, 0)))
    padded = jnp.concatenate([padded[:, :, -1:], padded, padded[:, :, :1]], axis=2)
    total = jnp.zeros((batch, rows_lat, cols_lon, chans), jnp.float32)
    for tap_index in range(9):
        row_step, col_step = divmod(tap_index, 3)
        window = padded[:, row_step:row_step + rows_lat, col_step:col_step + cols_lon, :].reshape(-1, chans)
        product = jnp.dot(window, kernel[tap_index], preferred_element_type=jnp.float32)
        total = total + product.reshape(batch, rows_lat, cols_lon, chans) * row_scales[None, :, None, tap_index, :]
    return total

def reference(latent, band_index, time_shift, norm_gains, tap_scale, conv_one, conv_two):
    first_scales = tap_scale[0][band_index]
    second_scales = tap_scale[1][band_index]
    first = norm_silu(latent.astype(jnp.float32), norm_gains[0])
    middle = convolve(first, conv_one, first_scales) + time_shift[:, None, None, :]
    second = norm_silu(middle, norm_gains[1])
    result = latent.astype(jnp.float32) + convolve(second, conv_two, second_scales)
    return result.astype(jnp.bfloat16)
```

```python
import functools

import jax
import jax.numpy as jnp
from jax import lax
from jax.experimental import pallas as pl
from jax.experimental.pallas import tpu as pltpu
from jax.sharding import PartitionSpec as P

NORM_GROUPS = 32
EPSILON = 1e-06
MESH = pl.DeviceIdType.MESH
F32 = jnp.float32
BF16 = jnp.bfloat16
WAYS = ((-1, 0), (1, 0), (0, -1), (0, 1), (-1, -1), (-1, 1), (1, -1), (1, 1))


def kernel(
    n_lon,
    n_lat,
    latent,
    band,
    time_shift,
    gains,
    tap_scale,
    conv_one,
    conv_two,
    out,
    field,
    act,
    weights,
    scales,
    row_halo,
    col_halo,
    corner_halo,
    col_send,
    corner_send,
    edge_act,
    stat_send,
    stat_recv,
    group_sum,
    weight_sem,
    halo_send_sem,
    halo_recv_sem,
    stat_send_sem,
    stat_recv_sem,
):
    batch, rows, cols, chans = latent.shape
    n = n_lon * n_lat
    per_group = chans // NORM_GROUPS
    local_count = float(rows * cols * per_group)
    whole_count = local_count * n
    lon = lax.axis_index("lon")
    lat = lax.axis_index("lat")
    me = lon * n_lat + lat

    def peer_id(step):
        peer = lax.rem(me + step, n)
        return {"lon": peer // n_lat, "lat": lax.rem(peer, n_lat)}

    barrier = pltpu.get_barrier_semaphore()

    @pl.loop(1, n)
    def _(step):
        pl.semaphore_signal(barrier, inc=1, device_id=peer_id(step), device_id_type=MESH)

    weight_copies = [
        pltpu.make_async_copy(src, weights.at[k], weight_sem.at[k])
        for k, src in enumerate((conv_one, conv_two))
    ]
    for copy in weight_copies:
        copy.start()

    def halo_copy(phase, b, way):
        d_lat, d_lon = WAYS[way]
        if d_lon == 0:
            top = d_lat < 0
            src = field.at[b, 0 if top else rows - 1]
            dst = row_halo.at[phase, b, 1 if top else 0]
        elif d_lat == 0:
            left = d_lon < 0
            src = col_send.at[phase, b, 0 if left else 1]
            dst = col_halo.at[phase, b, 1 if left else 0]
        else:
            mine = (0 if d_lat < 0 else 2) + (0 if d_lon < 0 else 1)
            src = corner_send.at[phase, b, mine]
            dst = corner_halo.at[phase, b, 3 - mine]
        return pltpu.make_async_remote_copy(
            src_ref=src,
            dst_ref=dst,
            send_sem=halo_send_sem.at[phase, b, way],
            recv_sem=halo_recv_sem.at[phase, b, way],
            device_id={
                "lon": lax.rem(lon + (d_lon + n_lon), n_lon),
                "lat": lat + d_lat,
            },
            device_id_type=MESH,
        )

    def when_lat(d_lat, body):
        if d_lat == 0:
            body()
        elif d_lat < 0:
            pl.when(lat > 0)(body)
        else:
            pl.when(lat < n_lat - 1)(body)

    def start_halos(phase, b):
        for side, col in ((0, 0), (1, cols - 1)):

            @pl.loop(0, rows)
            def _(r):
                col_send[phase, b, side, pl.ds(r, 1), :] = field[b, r, col : col + 1, :]

        for mine, (r, c) in enumerate(
            ((0, 0), (0, cols - 1), (rows - 1, 0), (rows - 1, cols - 1))
        ):
            corner_send[phase, b, mine] = field[b, r, c : c + 1, :]
        for way, (d_lat, _) in enumerate(WAYS):
            when_lat(d_lat, lambda way=way: halo_copy(phase, b, way).start())

    def wait_halos(phase, b):
        for way, (d_lat, _) in enumerate(WAYS):
            when_lat(d_lat, lambda way=way: halo_copy(phase, b, way).wait_send())
            when_lat(-d_lat, lambda way=way: halo_copy(phase, b, way).wait_recv())

    def over_group(per_chan):
        high = per_chan.astype(BF16).astype(F32)
        rest = per_chan - high
        middle = rest.astype(BF16).astype(F32)
        low = rest - middle
        line = lax.broadcasted_iota(jnp.int32, (16, chans), 0)
        parts = jnp.where(
            line == 0,
            high,
            jnp.where(line == 1, middle, jnp.where(line == 2, low, 0.0)),
        )
        summed = jnp.dot(parts.astype(BF16), group_sum[...], preferred_element_type=F32)
        return jnp.sum(summed, axis=0, keepdims=True)

    def fold(x):
        return jnp.sum(x.reshape(cols // 8, 8, chans), axis=0)

    def local_sum(b):
        def body(r, total):
            return total + fold(field[b, r])

        return lax.fori_loop(0, rows, body, jnp.zeros((8, chans), F32), unroll=4)

    def stat_copy(phase, b, step, span):
        return pltpu.make_async_remote_copy(
            src_ref=stat_send.at[phase, b] if span == 1 else stat_recv.at[phase, b, pl.ds(1, span)],
            dst_ref=stat_recv.at[phase, b, step]
            if span == 1
            else stat_recv.at[phase, b, pl.ds(1, span)],
            send_sem=stat_send_sem.at[phase, b],
            recv_sem=stat_recv_sem.at[phase, b],
            device_id=peer_id(step),
            device_id_type=MESH,
        )

    def local_stats(phase, b, total):
        summed = over_group(jnp.sum(total, axis=0, keepdims=True))
        average = summed * (1.0 / local_count)

        def body(r, squares):
            centred = field[b, r] - average
            return squares + fold(centred * centred)

        squares = lax.fori_loop(0, rows, body, jnp.zeros((8, chans), F32), unroll=4)
        squares = jnp.sum(squares, axis=0, keepdims=True)
        stat_send[phase, b, 0:1] = summed
        stat_send[phase, b, 1:2] = squares
        stat_recv[phase, b, 0, 0:1] = summed
        stat_recv[phase, b, 0, 1:2] = squares

    def start_stats(phase, b):
        @pl.loop(1, n)
        def _(step):
            stat_copy(phase, b, step, 1).start()

    def finish_stats(phase, b):
        stat_copy(phase, b, 1, n - 1).wait_recv()
        sums = stat_recv[phase, b, :, 0:1, :]
        squares = jnp.sum(stat_recv[phase, b, :, 1:2, :], axis=0)
        average = jnp.sum(sums, axis=0) * (1.0 / whole_count)
        apart = sums * (1.0 / local_count) - average[None]
        between = jnp.sum(apart * apart, axis=0) * local_count
        spread = (over_group(squares) + between) * (1.0 / whole_count)
        return average, lax.rsqrt(spread + EPSILON) * gains[phase : phase + 1, :] * 0.5

    def activate(phase, b, average, slope):
        def norm_silu(x):
            half = (x - average) * slope
            return half + half * jnp.tanh(half)

        for side in range(2):
            edge_act[side] = norm_silu(col_halo[phase, b, side])
        line = lax.broadcasted_iota(jnp.int32, (cols, chans), 0)

        def put(place, y, left, right):
            act[b, 1, place] = y.astype(BF16)
            before = jnp.where(line == 0, left, pltpu.roll(y, 1, axis=0))
            act[b, 0, place] = before.astype(BF16)
            after = jnp.where(line == cols - 1, right, pltpu.roll(y, cols - 1, axis=0))
            act[b, 2, place] = after.astype(BF16)

        @pl.loop(0, rows)
        def _(r):
            put(
                r + 1,
                norm_silu(field[b, r]),
                edge_act[0, pl.ds(r, 1), :],
                edge_act[1, pl.ds(r, 1), :],
            )

        for end, inside in ((0, lat > 0), (1, lat < n_lat - 1)):
            place = (rows + 1) * end

            @pl.when(inside)
            def _():
                put(
                    place,
                    norm_silu(row_halo[phase, b, end]),
                    norm_silu(corner_halo[phase, b, 2 * end]),
                    norm_silu(corner_halo[phase, b, 2 * end + 1]),
                )

            @pl.when(jnp.logical_not(inside))
            def _():
                for q in range(3):
                    act[b, q, place] = jnp.zeros((cols, chans), BF16)

    STEP = 8

    def convolve(k, b, finish):
        @pl.loop(0, rows // STEP)
        def _(chunk):
            base = chunk * STEP
            total = None
            for tap in range(9):
                p, q = divmod(tap, 3)
                window = act[b, q, pl.ds(base + p, STEP)].reshape(STEP * cols, chans)
                product = jnp.dot(window, weights[k, tap], preferred_element_type=F32)
                term = product.reshape(STEP, cols, chans) * scales[
                    k, pl.ds(base, STEP), tap : tap + 1, :
                ]
                total = term if total is None else total + term
            finish(base, total)

    def group_of(dim):
        index = lax.broadcasted_iota(jnp.int32, (chans, chans), dim).astype(F32)
        return jnp.floor((index + 0.5) * (1.0 / per_group))

    group_sum[...] = jnp.where(group_of(0) == group_of(1), 1.0, 0.0).astype(BF16)

    for k in range(2):

        @pl.loop(0, rows)
        def _(h):
            scales[k, h] = tap_scale[k, band[h]]

    for b in range(batch):

        def load_row(r, total, b=b):
            x = latent[b, r].astype(F32)
            field[b, r] = x
            return total + fold(x)

        total = lax.fori_loop(0, rows, load_row, jnp.zeros((8, chans), F32), unroll=4)
        if b == 0:
            pl.semaphore_wait(barrier, n - 1)
        start_halos(0, b)
        local_stats(0, b, total)
        start_stats(0, b)

    weight_copies[0].wait()
    for b in range(batch):
        average, slope = finish_stats(0, b)
        wait_halos(0, b)
        activate(0, b, average, slope)
        shift = time_shift[b : b + 1, :]

        def keep(base, total, b=b, shift=shift):
            field[b, pl.ds(base, STEP)] = total + shift[None]

        convolve(0, b, keep)
        start_halos(1, b)
        local_stats(1, b, local_sum(b))
        start_stats(1, b)

    weight_copies[1].wait()
    for b in range(batch):
        average, slope = finish_stats(1, b)
        wait_halos(1, b)
        activate(1, b, average, slope)

        def emit(base, total, b=b):
            place = pl.ds(base, STEP)
            out[b, place] = (latent[b, place].astype(F32) + total).astype(BF16)

        convolve(1, b, emit)

    for phase in range(2):
        for b in range(batch):
            stat_copy(phase, b, 1, n - 1).wait_send()


def solution(mesh):
    n_lon, n_lat = mesh.shape["lon"], mesh.shape["lat"]
    n = n_lon * n_lat

    def local(latent, band_index, time_shift, norm_gains, tap_scale, conv_one, conv_two):
        batch, rows, cols, chans = latent.shape
        taps = conv_one.shape[0]
        vmem = pl.BlockSpec(memory_space=pltpu.VMEM)
        smem = pl.BlockSpec(memory_space=pltpu.SMEM)
        anywhere = pl.BlockSpec(memory_space=pl.ANY)
        dma = pltpu.SemaphoreType.DMA
        return pl.pallas_call(
            functools.partial(kernel, n_lon, n_lat),
            out_shape=jax.ShapeDtypeStruct(latent.shape, latent.dtype),
            in_specs=[vmem, smem, vmem, vmem, vmem, anywhere, anywhere],
            out_specs=vmem,
            scratch_shapes=[
                pltpu.VMEM((batch, rows, cols, chans), F32),
                pltpu.VMEM((batch, 3, rows + 2, cols, chans), BF16),
                pltpu.VMEM((2, taps, chans, chans), BF16),
                pltpu.VMEM((2, rows, taps, chans), F32),
                pltpu.VMEM((2, batch, 2, cols, chans), F32),
                pltpu.VMEM((2, batch, 2, rows, chans), F32),
                pltpu.VMEM((2, batch, 4, 1, chans), F32),
                pltpu.VMEM((2, batch, 2, rows, chans), F32),
                pltpu.VMEM((2, batch, 4, 1, chans), F32),
                pltpu.VMEM((2, rows, chans), F32),
                pltpu.VMEM((2, batch, 2, chans), F32),
                pltpu.VMEM((2, batch, n, 2, chans), F32),
                pltpu.VMEM((chans, chans), BF16),
                dma((2,)),
                dma((2, batch, 8)),
                dma((2, batch, 8)),
                dma((2, batch)),
                dma((2, batch)),
            ],
            compiler_params=pltpu.CompilerParams(
                collective_id=0, has_side_effects=True, vmem_limit_bytes=48 * 1024 * 1024
            ),
            name="block",
        )(latent, band_index, time_shift, norm_gains, tap_scale, conv_one, conv_two)

    return jax.shard_map(
        local,
        mesh=mesh,
        in_specs=(P("groups", "lat", "lon", None), P("lat"), P("groups", None), P(), P(), P(), P()),
        out_specs=P("groups", "lat", "lon", None),
        check_vma=False,
    )
```

```python
import functools

import jax
import jax.numpy as jnp
from jax import lax
from jax.experimental import pallas as pl
from jax.experimental.pallas import tpu as pltpu
from jax.sharding import PartitionSpec as P

NORM_GROUPS = 32
EPSILON = 1e-06
MESH = pl.DeviceIdType.MESH
F32 = jnp.float32
BF16 = jnp.bfloat16
WIDE = 256
REST = 64
STEP = 24
WAYS = ((-1, 0), (1, 0), (0, -1), (0, 1), (-1, -1), (-1, 1), (1, -1), (1, 1))


def kernel(
    n_lon,
    n_lat,
    latent_hbm,
    band_hbm,
    time_shift_hbm,
    gains_hbm,
    tap_scale_hbm,
    conv_one,
    conv_two,
    out,
    latent,
    band,
    time_shift,
    gains,
    tap_scale,
    table,
    tails,
    field,
    act,
    weights,
    scales,
    row_halo,
    col_halo,
    corner_halo,
    col_send,
    corner_send,
    edge_act,
    stat_send,
    stat_recv,
    group_sum,
    load_sem,
    weight_sem,
    halo_send_sem,
    halo_recv_sem,
    stat_send_sem,
    stat_recv_sem,
):
    batch, rows, cols, chans = latent.shape
    n = n_lon * n_lat
    per_group = chans // NORM_GROUPS
    local_count = float(rows * cols * per_group)
    whole_count = local_count * n
    lon = lax.axis_index("lon")
    lat = lax.axis_index("lat")
    me = lon * n_lat + lat

    def peer_id(step):
        peer = lax.rem(me + step, n)
        return {"lon": peer // n_lat, "lat": lax.rem(peer, n_lat)}

    loads = [
        pltpu.make_async_copy(src, dst, load_sem.at[i])
        for i, (src, dst) in enumerate(
            [(latent_hbm.at[b], latent.at[b]) for b in range(batch)]
            + [
                (tap_scale_hbm, tap_scale),
                (band_hbm, band),
                (gains_hbm, gains),
                (time_shift_hbm, time_shift),
            ]
        )
    ]
    for copy in loads:
        copy.start()

    barrier = pltpu.get_barrier_semaphore()

    @pl.loop(1, n)
    def _(step):
        pl.semaphore_signal(barrier, inc=1, device_id=peer_id(step), device_id_type=MESH)

    weight_copies = [
        pltpu.make_async_copy(src, weights.at[k], weight_sem.at[k])
        for k, src in enumerate((conv_one, conv_two))
    ]
    for copy in weight_copies:
        copy.start()

    def halo_copy(phase, b, way):
        d_lat, d_lon = WAYS[way]
        if d_lon == 0:
            top = d_lat < 0
            src = field.at[b, 0 if top else rows - 1]
            dst = row_halo.at[phase, b, 1 if top else 0]
        elif d_lat == 0:
            left = d_lon < 0
            src = col_send.at[phase, b, 0 if left else 1]
            dst = col_halo.at[phase, b, 1 if left else 0]
        else:
            mine = (0 if d_lat < 0 else 2) + (0 if d_lon < 0 else 1)
            src = corner_send.at[phase, b, mine]
            dst = corner_halo.at[phase, b, 3 - mine]
        return pltpu.make_async_remote_copy(
            src_ref=src,
            dst_ref=dst,
            send_sem=halo_send_sem.at[phase, b, way],
            recv_sem=halo_recv_sem.at[phase, b, way],
            device_id={
                "lon": lax.rem(lon + (d_lon + n_lon), n_lon),
                "lat": lat + d_lat,
            },
            device_id_type=MESH,
        )

    def when_lat(d_lat, body):
        if d_lat == 0:
            body()
        elif d_lat < 0:
            pl.when(lat > 0)(body)
        else:
            pl.when(lat < n_lat - 1)(body)

    def start_halos(phase, b):
        for side, col in ((0, 0), (1, cols - 1)):

            @pl.loop(0, rows, unroll=8)
            def _(r):
                col_send[phase, b, side, pl.ds(r, 1), :] = field[b, r, col : col + 1, :]

        for mine, (r, c) in enumerate(
            ((0, 0), (0, cols - 1), (rows - 1, 0), (rows - 1, cols - 1))
        ):
            corner_send[phase, b, mine] = field[b, r, c : c + 1, :]
        if phase == 0 and b == 0:
            pl.semaphore_wait(barrier, n - 1)
        for way, (d_lat, _) in enumerate(WAYS):
            when_lat(d_lat, lambda way=way: halo_copy(phase, b, way).start())

    def wait_halos(phase, b):
        for way, (d_lat, _) in enumerate(WAYS):
            when_lat(d_lat, lambda way=way: halo_copy(phase, b, way).wait_send())
            when_lat(-d_lat, lambda way=way: halo_copy(phase, b, way).wait_recv())

    def over_group(per_chan):
        high = per_chan.astype(BF16).astype(F32)
        rest = per_chan - high
        middle = rest.astype(BF16).astype(F32)
        low = rest - middle
        line = lax.broadcasted_iota(jnp.int32, (16, chans), 0)
        parts = jnp.where(
            line == 0,
            high,
            jnp.where(line == 1, middle, jnp.where(line == 2, low, 0.0)),
        )
        summed = jnp.dot(parts.astype(BF16), group_sum[...], preferred_element_type=F32)
        return jnp.sum(summed, axis=0, keepdims=True)

    def fold(x):
        return jnp.sum(x.reshape(cols // 8, 8, chans), axis=0)

    def local_sum(b):
        def body(r, total):
            return total + fold(field[b, r])

        return lax.fori_loop(0, rows, body, jnp.zeros((8, chans), F32), unroll=4)

    def stat_copy(phase, b, step, span):
        return pltpu.make_async_remote_copy(
            src_ref=stat_send.at[phase, b] if span == 1 else stat_recv.at[phase, b, pl.ds(1, span)],
            dst_ref=stat_recv.at[phase, b, step]
            if span == 1
            else stat_recv.at[phase, b, pl.ds(1, span)],
            send_sem=stat_send_sem.at[phase, b],
            recv_sem=stat_recv_sem.at[phase, b],
            device_id=peer_id(step),
            device_id_type=MESH,
        )

    def local_stats(phase, b, total):
        summed = over_group(jnp.sum(total, axis=0, keepdims=True))
        average = summed * (1.0 / local_count)

        def body(r, squares):
            centred = field[b, r] - average
            return squares + fold(centred * centred)

        squares = lax.fori_loop(0, rows, body, jnp.zeros((8, chans), F32), unroll=4)
        squares = jnp.sum(squares, axis=0, keepdims=True)
        stat_send[phase, b, 0:1] = summed
        stat_send[phase, b, 1:2] = squares
        stat_recv[phase, b, 0, 0:1] = summed
        stat_recv[phase, b, 0, 1:2] = squares

    def start_stats(phase, b):
        @pl.loop(1, n)
        def _(step):
            stat_copy(phase, b, step, 1).start()

    def finish_stats(phase, b):
        stat_copy(phase, b, 1, n - 1).wait_recv()
        sums = stat_recv[phase, b, :, 0:1, :]
        squares = jnp.sum(stat_recv[phase, b, :, 1:2, :], axis=0)
        average = jnp.sum(sums, axis=0) * (1.0 / whole_count)
        apart = sums * (1.0 / local_count) - average[None]
        between = jnp.sum(apart * apart, axis=0) * local_count
        spread = (over_group(squares) + between) * (1.0 / whole_count)
        return average, lax.rsqrt(spread + EPSILON) * gains[phase : phase + 1, :] * 0.5

    def activate(phase, b, average, slope):
        def norm_silu(x):
            half = (x - average) * slope
            return half + half * jnp.tanh(half)

        for side in range(2):
            edge_act[side] = norm_silu(col_halo[phase, b, side])
        line = lax.broadcasted_iota(jnp.int32, (cols, chans), 0)

        def put(place, y, left, right):
            act[b, 1, place] = y.astype(BF16)
            before = jnp.where(line == 0, left, pltpu.roll(y, 1, axis=0))
            act[b, 0, place] = before.astype(BF16)
            after = jnp.where(line == cols - 1, right, pltpu.roll(y, cols - 1, axis=0))
            act[b, 2, place] = after.astype(BF16)

        @pl.loop(0, rows, unroll=2)
        def _(r):
            put(
                r + 1,
                norm_silu(field[b, r]),
                edge_act[0, pl.ds(r, 1), :],
                edge_act[1, pl.ds(r, 1), :],
            )

        for end, inside in ((0, lat > 0), (1, lat < n_lat - 1)):
            place = (rows + 1) * end

            @pl.when(inside)
            def _():
                put(
                    place,
                    norm_silu(row_halo[phase, b, end]),
                    norm_silu(corner_halo[phase, b, 2 * end]),
                    norm_silu(corner_halo[phase, b, 2 * end + 1]),
                )

            @pl.when(jnp.logical_not(inside))
            def _():
                for q in range(3):
                    act[b, q, place] = jnp.zeros((cols, chans), BF16)

    def convolve(k, b, finish):
        @pl.loop(0, rows // STEP)
        def _(chunk):
            base = chunk * STEP

            def scale(tap, low, high):
                return scales[k, pl.ds(base, STEP), tap : tap + 1, low:high]

            body = even = odd = None
            for q in range(3):
                for p in range(3):
                    window = act[b, q, pl.ds(base + p, STEP)].reshape(STEP * cols, chans)
                    product = jnp.dot(
                        window, weights[k, 3 * p + q, :, :WIDE], preferred_element_type=F32
                    )
                    term = product.reshape(STEP, cols, WIDE) * scale(3 * p + q, 0, WIDE)
                    body = term if body is None else body + term
                window = act[b, q, pl.ds(base, STEP + 2)].reshape((STEP + 2) * cols, chans)
                product = jnp.dot(window, tails[k, q], preferred_element_type=F32)
                product = product.reshape(STEP + 2, cols, 4 * REST)
                side = [scale(3 * p + q, WIDE, WIDE + 2 * REST) for p in range(3)]
                ends = (
                    product[:STEP, :, : 2 * REST] * side[0]
                    + product[2:, :, 2 * REST :] * side[2]
                )
                mid = product[1 : STEP + 1, :, : 2 * REST] * side[1]
                even = ends if even is None else even + ends
                odd = mid if odd is None else odd + mid
            odd = pltpu.roll(odd.reshape(STEP * cols, 2 * REST), REST, axis=1)
            rest = (even + odd.reshape(STEP, cols, 2 * REST))[:, :, :REST]
            finish(base, jnp.concatenate([body, rest], axis=-1))

    def group_of(dim):
        index = lax.broadcasted_iota(jnp.int32, (chans, chans), dim).astype(F32)
        return jnp.floor((index + 0.5) * (1.0 / per_group))

    group_sum[...] = jnp.where(group_of(0) == group_of(1), 1.0, 0.0).astype(BF16)

    for b in range(batch):
        loads[b].wait()

        def load_row(r, total, b=b):
            x = latent[b, r].astype(F32)
            field[b, r] = x
            return total + fold(x)

        total = lax.fori_loop(0, rows, load_row, jnp.zeros((8, chans), F32), unroll=4)
        start_halos(0, b)
        local_stats(0, b, total)
        start_stats(0, b)

    for copy in loads[batch:]:
        copy.wait()
    for k in range(2):
        for tap in range(9):
            lines = tap_scale[k, tap]
            lines = jnp.concatenate([lines, lines[:, WIDE:]], axis=1)
            for line in range(lines.shape[0]):
                table[k, line, tap : tap + 1] = lines[line : line + 1]

        @pl.loop(0, rows, unroll=4)
        def _(h):
            scales[k, h] = table[k, band[h]]

        weight_copies[k].wait()
        for q in range(3):
            parts = [weights[k, 3 * p + q, :, WIDE:] for p in range(3)]
            tails[k, q] = jnp.concatenate(parts + [jnp.zeros((chans, REST), BF16)], axis=1)

    for b in range(batch):
        average, slope = finish_stats(0, b)
        wait_halos(0, b)
        activate(0, b, average, slope)
        shift = time_shift[b : b + 1, :]

        def keep(base, total, b=b, shift=shift):
            field[b, pl.ds(base, STEP)] = total + shift[None]

        convolve(0, b, keep)
        start_halos(1, b)
        local_stats(1, b, local_sum(b))
        start_stats(1, b)

    for b in range(batch):
        average, slope = finish_stats(1, b)
        wait_halos(1, b)
        activate(1, b, average, slope)

        def emit(base, total, b=b):
            place = pl.ds(base, STEP)
            out[b, place] = (latent[b, place].astype(F32) + total).astype(BF16)

        convolve(1, b, emit)

    for phase in range(2):
        for b in range(batch):
            stat_copy(phase, b, 1, n - 1).wait_send()


def solution(mesh):
    n_lon, n_lat = mesh.shape["lon"], mesh.shape["lat"]
    n = n_lon * n_lat

    def local(latent, band_index, time_shift, norm_gains, tap_scale, conv_one, conv_two):
        batch, rows, cols, chans = latent.shape
        taps = conv_one.shape[0]
        vmem = pl.BlockSpec(memory_space=pltpu.VMEM)
        hbm = pl.BlockSpec(memory_space=pltpu.HBM)
        bands = tap_scale.shape[1]
        dma = pltpu.SemaphoreType.DMA
        by_tap = jnp.transpose(tap_scale, (0, 2, 1, 3))
        return pl.pallas_call(
            functools.partial(kernel, n_lon, n_lat),
            out_shape=jax.ShapeDtypeStruct(latent.shape, latent.dtype),
            in_specs=[hbm] * 7,
            out_specs=vmem,
            scratch_shapes=[
                pltpu.VMEM(latent.shape, BF16),
                pltpu.SMEM(band_index.shape, jnp.int32),
                pltpu.VMEM(time_shift.shape, F32),
                pltpu.VMEM(norm_gains.shape, F32),
                pltpu.VMEM((2, taps, bands, chans), F32),
                pltpu.VMEM((2, bands, taps, WIDE + 2 * REST), F32),
                pltpu.VMEM((2, 3, chans, 4 * REST), BF16),
                pltpu.VMEM((batch, rows, cols, chans), F32),
                pltpu.VMEM((batch, 3, rows + 2, cols, chans), BF16),
                pltpu.VMEM((2, taps, chans, chans), BF16),
                pltpu.VMEM((2, rows, taps, WIDE + 2 * REST), F32),
                pltpu.VMEM((2, batch, 2, cols, chans), F32),
                pltpu.VMEM((2, batch, 2, rows, chans), F32),
                pltpu.VMEM((2, batch, 4, 1, chans), F32),
                pltpu.VMEM((2, batch, 2, rows, chans), F32),
                pltpu.VMEM((2, batch, 4, 1, chans), F32),
                pltpu.VMEM((2, rows, chans), F32),
                pltpu.VMEM((2, batch, 2, chans), F32),
                pltpu.VMEM((2, batch, n, 2, chans), F32),
                pltpu.VMEM((chans, chans), BF16),
                dma((batch + 4,)),
                dma((2,)),
                dma((2, batch, 8)),
                dma((2, batch, 8)),
                dma((2, batch)),
                dma((2, batch)),
            ],
            compiler_params=pltpu.CompilerParams(
                collective_id=0, has_side_effects=True, vmem_limit_bytes=int(62 * 1024 * 1024)
            ),
            name="block",
        )(latent, band_index, time_shift, norm_gains, by_tap, conv_one, conv_two)

    return jax.shard_map(
        local,
        mesh=mesh,
        in_specs=(P("groups", "lat", "lon", None), P("lat"), P("groups", None), P(), P(), P(), P()),
        out_specs=P("groups", "lat", "lon", None),
        check_vma=False,
    )
```

```python
import functools

import jax
import jax.numpy as jnp
from jax import lax
from jax.experimental import pallas as pl
from jax.experimental.pallas import tpu as pltpu
from jax.sharding import PartitionSpec as P

NORM_GROUPS = 32
EPSILON = 1e-06
MESH = pl.DeviceIdType.MESH
F32 = jnp.float32
BF16 = jnp.bfloat16
WIDE = 256
REST = 64
STEP = 24
WAYS = ((-1, 0), (1, 0), (0, -1), (0, 1), (-1, -1), (-1, 1), (1, -1), (1, 1))


def kernel(
    n_lon,
    n_lat,
    latent_hbm,
    band_hbm,
    time_shift_hbm,
    gains_hbm,
    tap_scale_hbm,
    conv_one,
    conv_two,
    out,
    latent,
    band,
    time_shift,
    gains,
    tap_scale,
    table,
    tails,
    field,
    act,
    weights,
    scales,
    row_halo,
    col_halo,
    corner_halo,
    col_send,
    corner_send,
    edge_act,
    stat_send,
    stat_recv,
    group_sum,
    load_sem,
    store_sem,
    weight_sem,
    halo_send_sem,
    halo_recv_sem,
    stat_send_sem,
    stat_recv_sem,
):
    batch, rows, cols, chans = latent.shape
    n = n_lon * n_lat
    per_group = chans // NORM_GROUPS
    local_count = float(rows * cols * per_group)
    whole_count = local_count * n
    lon = lax.axis_index("lon")
    lat = lax.axis_index("lat")
    me = lon * n_lat + lat

    def peer_id(step):
        peer = lax.rem(me + step, n)
        return {"lon": peer // n_lat, "lat": lax.rem(peer, n_lat)}

    loads = [
        pltpu.make_async_copy(src, dst, load_sem.at[i])
        for i, (src, dst) in enumerate(
            [(latent_hbm.at[b], latent.at[b]) for b in range(batch)]
            + [
                (tap_scale_hbm, tap_scale),
                (band_hbm, band),
                (gains_hbm, gains),
                (time_shift_hbm, time_shift),
            ]
        )
    ]
    for copy in loads:
        copy.start()

    barrier = pltpu.get_barrier_semaphore()

    @pl.loop(1, n)
    def _(step):
        pl.semaphore_signal(barrier, inc=1, device_id=peer_id(step), device_id_type=MESH)

    stores = [
        pltpu.make_async_copy(latent.at[b], out.at[b], store_sem.at[b]) for b in range(batch)
    ]
    weight_copies = [
        pltpu.make_async_copy(src, weights.at[k], weight_sem.at[k])
        for k, src in enumerate((conv_one, conv_two))
    ]
    for copy in weight_copies:
        copy.start()

    def halo_copy(phase, b, way):
        d_lat, d_lon = WAYS[way]
        if d_lon == 0:
            top = d_lat < 0
            src = field.at[b, 0 if top else rows - 1]
            dst = row_halo.at[phase, b, 1 if top else 0]
        elif d_lat == 0:
            left = d_lon < 0
            src = col_send.at[phase, b, 0 if left else 1]
            dst = col_halo.at[phase, b, 1 if left else 0]
        else:
            mine = (0 if d_lat < 0 else 2) + (0 if d_lon < 0 else 1)
            src = corner_send.at[phase, b, mine]
            dst = corner_halo.at[phase, b, 3 - mine]
        return pltpu.make_async_remote_copy(
            src_ref=src,
            dst_ref=dst,
            send_sem=halo_send_sem.at[phase, b, way],
            recv_sem=halo_recv_sem.at[phase, b, way],
            device_id={
                "lon": lax.rem(lon + (d_lon + n_lon), n_lon),
                "lat": lat + d_lat,
            },
            device_id_type=MESH,
        )

    def when_lat(d_lat, body):
        if d_lat == 0:
            body()
        elif d_lat < 0:
            pl.when(lat > 0)(body)
        else:
            pl.when(lat < n_lat - 1)(body)

    def start_halos(phase, b):
        for side, col in ((0, 0), (1, cols - 1)):

            @pl.loop(0, rows, unroll=8)
            def _(r):
                col_send[phase, b, side, pl.ds(r, 1), :] = field[b, r, col : col + 1, :]

        for mine, (r, c) in enumerate(
            ((0, 0), (0, cols - 1), (rows - 1, 0), (rows - 1, cols - 1))
        ):
            corner_send[phase, b, mine] = field[b, r, c : c + 1, :]
        if phase == 0 and b == 0:
            pl.semaphore_wait(barrier, n - 1)
        for way, (d_lat, _) in enumerate(WAYS):
            when_lat(d_lat, lambda way=way: halo_copy(phase, b, way).start())

    def wait_halos(phase, b):
        for way, (d_lat, _) in enumerate(WAYS):
            when_lat(d_lat, lambda way=way: halo_copy(phase, b, way).wait_send())
            when_lat(-d_lat, lambda way=way: halo_copy(phase, b, way).wait_recv())

    def over_group(per_chan):
        high = per_chan.astype(BF16).astype(F32)
        rest = per_chan - high
        middle = rest.astype(BF16).astype(F32)
        low = rest - middle
        line = lax.broadcasted_iota(jnp.int32, (16, chans), 0)
        parts = jnp.where(
            line == 0,
            high,
            jnp.where(line == 1, middle, jnp.where(line == 2, low, 0.0)),
        )
        summed = jnp.dot(parts.astype(BF16), group_sum[...], preferred_element_type=F32)
        return jnp.sum(summed, axis=0, keepdims=True)

    def fold(x):
        return jnp.sum(x.reshape(cols // 8, 8, chans), axis=0)

    def local_sum(b):
        def body(r, total):
            return total + fold(field[b, r])

        return lax.fori_loop(0, rows, body, jnp.zeros((8, chans), F32), unroll=8)

    def stat_copy(phase, b, step, span):
        return pltpu.make_async_remote_copy(
            src_ref=stat_send.at[phase, b] if span == 1 else stat_recv.at[phase, b, pl.ds(1, span)],
            dst_ref=stat_recv.at[phase, b, step]
            if span == 1
            else stat_recv.at[phase, b, pl.ds(1, span)],
            send_sem=stat_send_sem.at[phase, b],
            recv_sem=stat_recv_sem.at[phase, b],
            device_id=peer_id(step),
            device_id_type=MESH,
        )

    def local_stats(phase, b, total):
        summed = over_group(jnp.sum(total, axis=0, keepdims=True))
        average = summed * (1.0 / local_count)

        def body(r, squares):
            centred = field[b, r] - average
            return squares + fold(centred * centred)

        squares = lax.fori_loop(0, rows, body, jnp.zeros((8, chans), F32), unroll=8)
        squares = jnp.sum(squares, axis=0, keepdims=True)
        stat_send[phase, b, 0:1] = summed
        stat_send[phase, b, 1:2] = squares
        stat_recv[phase, b, 0, 0:1] = summed
        stat_recv[phase, b, 0, 1:2] = squares

    def start_stats(phase, b):
        @pl.loop(1, n)
        def _(step):
            stat_copy(phase, b, step, 1).start()

    def finish_stats(phase, b):
        stat_copy(phase, b, 1, n - 1).wait_recv()
        sums = stat_recv[phase, b, :, 0:1, :]
        squares = jnp.sum(stat_recv[phase, b, :, 1:2, :], axis=0)
        average = jnp.sum(sums, axis=0) * (1.0 / whole_count)
        apart = sums * (1.0 / local_count) - average[None]
        between = jnp.sum(apart * apart, axis=0) * local_count
        spread = (over_group(squares) + between) * (1.0 / whole_count)
        return average, lax.rsqrt(spread + EPSILON) * gains[phase : phase + 1, :] * 0.5

    def activate(phase, b, average, slope):
        def norm_silu(x):
            half = (x - average) * slope
            return half + half * jnp.tanh(half)

        for side in range(2):
            edge_act[side] = norm_silu(col_halo[phase, b, side])
        line = lax.broadcasted_iota(jnp.int32, (cols, chans), 0)

        def put(place, y, left, right):
            act[b, 1, place] = y.astype(BF16)
            before = jnp.where(line == 0, left, pltpu.roll(y, 1, axis=0))
            act[b, 0, place] = before.astype(BF16)
            after = jnp.where(line == cols - 1, right, pltpu.roll(y, cols - 1, axis=0))
            act[b, 2, place] = after.astype(BF16)

        @pl.loop(0, rows, unroll=6)
        def _(r):
            put(
                r + 1,
                norm_silu(field[b, r]),
                edge_act[0, pl.ds(r, 1), :],
                edge_act[1, pl.ds(r, 1), :],
            )

        for end, inside in ((0, lat > 0), (1, lat < n_lat - 1)):
            place = (rows + 1) * end

            @pl.when(inside)
            def _():
                put(
                    place,
                    norm_silu(row_halo[phase, b, end]),
                    norm_silu(corner_halo[phase, b, 2 * end]),
                    norm_silu(corner_halo[phase, b, 2 * end + 1]),
                )

            @pl.when(jnp.logical_not(inside))
            def _():
                for q in range(3):
                    act[b, q, place] = jnp.zeros((cols, chans), BF16)

    def convolve(k, b, finish):
        @pl.loop(0, rows // STEP)
        def _(chunk):
            base = chunk * STEP

            def scale(tap, low, high):
                return scales[k, pl.ds(base, STEP), tap : tap + 1, low:high]

            body = even = odd = None
            for q in range(3):
                for p in range(3):
                    window = act[b, q, pl.ds(base + p, STEP)].reshape(STEP * cols, chans)
                    product = jnp.dot(
                        window, weights[k, 3 * p + q, :, :WIDE], preferred_element_type=F32
                    )
                    term = product.reshape(STEP, cols, WIDE) * scale(3 * p + q, 0, WIDE)
                    body = term if body is None else body + term
                window = act[b, q, pl.ds(base, STEP + 2)].reshape((STEP + 2) * cols, chans)
                product = jnp.dot(window, tails[k, q], preferred_element_type=F32)
                product = product.reshape(STEP + 2, cols, 4 * REST)
                side = [scale(3 * p + q, WIDE, WIDE + 2 * REST) for p in range(3)]
                ends = (
                    product[:STEP, :, : 2 * REST] * side[0]
                    + product[2:, :, 2 * REST :] * side[2]
                )
                mid = product[1 : STEP + 1, :, : 2 * REST] * side[1]
                even = ends if even is None else even + ends
                odd = mid if odd is None else odd + mid
            odd = pltpu.roll(odd.reshape(STEP * cols, 2 * REST), REST, axis=1)
            rest = (even + odd.reshape(STEP, cols, 2 * REST))[:, :, :REST]
            finish(base, jnp.concatenate([body, rest], axis=-1))

    def group_of(dim):
        index = lax.broadcasted_iota(jnp.int32, (chans, chans), dim).astype(F32)
        return jnp.floor((index + 0.5) * (1.0 / per_group))

    group_sum[...] = jnp.where(group_of(0) == group_of(1), 1.0, 0.0).astype(BF16)

    for b in range(batch):
        loads[b].wait()

        def load_row(r, total, b=b):
            x = latent[b, r].astype(F32)
            field[b, r] = x
            return total + fold(x)

        total = lax.fori_loop(0, rows, load_row, jnp.zeros((8, chans), F32), unroll=8)
        start_halos(0, b)
        local_stats(0, b, total)
        start_stats(0, b)

    for copy in loads[batch:]:
        copy.wait()
    for k in range(2):
        for tap in range(9):
            lines = tap_scale[k, tap]
            lines = jnp.concatenate([lines, lines[:, WIDE:]], axis=1)
            for line in range(lines.shape[0]):
                table[k, line, tap : tap + 1] = lines[line : line + 1]

        @pl.loop(0, rows, unroll=8)
        def _(h):
            scales[k, h] = table[k, band[h]]

        weight_copies[k].wait()
        for q in range(3):
            parts = [weights[k, 3 * p + q, :, WIDE:] for p in range(3)]
            tails[k, q] = jnp.concatenate(parts + [jnp.zeros((chans, REST), BF16)], axis=1)

    for b in range(batch):
        average, slope = finish_stats(0, b)
        wait_halos(0, b)
        activate(0, b, average, slope)
        shift = time_shift[b : b + 1, :]

        def keep(base, total, b=b, shift=shift):
            field[b, pl.ds(base, STEP)] = total + shift[None]

        convolve(0, b, keep)
        start_halos(1, b)
        local_stats(1, b, local_sum(b))
        start_stats(1, b)

    for b in range(batch):
        average, slope = finish_stats(1, b)
        wait_halos(1, b)
        activate(1, b, average, slope)

        def emit(base, total, b=b):
            place = pl.ds(base, STEP)
            latent[b, place] = (latent[b, place].astype(F32) + total).astype(BF16)

        convolve(1, b, emit)
        stores[b].start()

    for phase in range(2):
        for b in range(batch):
            stat_copy(phase, b, 1, n - 1).wait_send()
    for copy in stores:
        copy.wait()


def solution(mesh):
    n_lon, n_lat = mesh.shape["lon"], mesh.shape["lat"]
    n = n_lon * n_lat

    def local(latent, band_index, time_shift, norm_gains, tap_scale, conv_one, conv_two):
        batch, rows, cols, chans = latent.shape
        taps = conv_one.shape[0]
        hbm = pl.BlockSpec(memory_space=pltpu.HBM)
        bands = tap_scale.shape[1]
        dma = pltpu.SemaphoreType.DMA
        by_tap = jnp.transpose(tap_scale, (0, 2, 1, 3))
        return pl.pallas_call(
            functools.partial(kernel, n_lon, n_lat),
            out_shape=jax.ShapeDtypeStruct(latent.shape, latent.dtype),
            in_specs=[hbm] * 7,
            out_specs=hbm,
            scratch_shapes=[
                pltpu.VMEM(latent.shape, BF16),
                pltpu.SMEM(band_index.shape, jnp.int32),
                pltpu.VMEM(time_shift.shape, F32),
                pltpu.VMEM(norm_gains.shape, F32),
                pltpu.VMEM((2, taps, bands, chans), F32),
                pltpu.VMEM((2, bands, taps, WIDE + 2 * REST), F32),
                pltpu.VMEM((2, 3, chans, 4 * REST), BF16),
                pltpu.VMEM((batch, rows, cols, chans), F32),
                pltpu.VMEM((batch, 3, rows + 2, cols, chans), BF16),
                pltpu.VMEM((2, taps, chans, chans), BF16),
                pltpu.VMEM((2, rows, taps, WIDE + 2 * REST), F32),
                pltpu.VMEM((2, batch, 2, cols, chans), F32),
                pltpu.VMEM((2, batch, 2, rows, chans), F32),
                pltpu.VMEM((2, batch, 4, 1, chans), F32),
                pltpu.VMEM((2, batch, 2, rows, chans), F32),
                pltpu.VMEM((2, batch, 4, 1, chans), F32),
                pltpu.VMEM((2, rows, chans), F32),
                pltpu.VMEM((2, batch, 2, chans), F32),
                pltpu.VMEM((2, batch, n, 2, chans), F32),
                pltpu.VMEM((chans, chans), BF16),
                dma((batch + 4,)),
                dma((batch,)),
                dma((2,)),
                dma((2, batch, 8)),
                dma((2, batch, 8)),
                dma((2, batch)),
                dma((2, batch)),
            ],
            compiler_params=pltpu.CompilerParams(
                collective_id=0, has_side_effects=True, vmem_limit_bytes=int(62 * 1024 * 1024)
            ),
            name="block",
        )(latent, band_index, time_shift, norm_gains, by_tap, conv_one, conv_two)

    return jax.shard_map(
        local,
        mesh=mesh,
        in_specs=(P("groups", "lat", "lon", None), P("lat"), P("groups", None), P(), P(), P(), P()),
        out_specs=P("groups", "lat", "lon", None),
        check_vma=False,
    )
```
